32 devices in a mesh: island: 8 (over z, x), tensor: 4 (over y, core).
Axes of the slice: x: 2, y: 2, z: 4, core: 2. Of those that a mesh axis runs over, the one named last changes fastest.
Arguments:
- hidden: bfloat16 [8, 512, 14336], P('island', None, 'tensor'), may hold values from -6 to 6
- island_weights: bfloat16 [8, 4096, 14336], P('island', None, 'tensor'), may hold values from -6 to 6
- targets: bfloat16 [8, 4096, 512], P('island', 'tensor'), may hold values from -6 to 6
- global_weights: float32 [1024, 14336], P('island', 'tensor'), may hold values from -6 to 6
- momentum: float32 [1024, 14336], P('island', 'tensor'), may hold values from -3 to 3
Outputs:
- mixed: bfloat16 [8, 1024, 14336], P('island', None, 'tensor')
- new_global: float32 [1024, 14336], P('island', 'tensor')
- new_momentum: float32 [1024, 14336], P('island', 'tensor')
- grad_hidden: bfloat16 [8, 512, 14336], P('island', None, 'tensor')
The draws below stay inside these ranges and needn't reach their ends.
All inputs are finite; a program needn't handle non-finite values.
Results may differ from the reference program's by a relative error of at most 0.015.
Values may be sent and summed in bfloat16 or wider, within the bound.
No kernel may reach another device: no remote copies, remote signals or barrier semaphores. Data moves between devices by JAX's collectives and lax.ppermute only.
A program may use at most 192 MiB of HBM per device.

```python
import math
import jax
import jax.numpy as jnp
from jax import lax

D = 4096
FF = 14336
FRAG = 1024
TOK = 512
ISL = 8


def spiked(result, rng, source, target, parts, factor):
    def block_of(dim):
        return (jnp.arange(result.shape[dim]) // (result.shape[dim] // parts)).reshape((-1,) + (1,) * (result.ndim - 1 - dim))

    first = jax.random.permutation(rng, parts)[block_of(target)]
    far = (block_of(target) + parts // 2) % parts
    return jnp.where((block_of(source) == first) | (block_of(source) == far), factor * result, result)


def shard_levels(rng, shape, split, least, largest):
    def one(dim, shards_of):
        steps = jax.random.uniform(jax.random.fold_in(jax.random.fold_in(rng, 6), dim), (shards_of,), jnp.float32, least / len(split), largest / len(split))
        return jnp.repeat(jnp.exp(steps), shape[dim] // shards_of).reshape((-1,) + (1,) * (len(shape) - dim - 1))

    loudness = one(*split[0])
    for cut in split[1:]:
        loudness = loudness * one(*cut)
    return loudness


def gaussian(key, dims, scale, reach, pieces=(), dtype=jnp.bfloat16):
    gain = shard_levels(key, dims, pieces, -0.22, 0.18) if pieces else 1.0
    values = jax.random.normal(key, dims, jnp.float32) * scale * gain
    return jnp.minimum(jnp.maximum(values, -reach), reach).astype(dtype)


def bell_draw_with(own_key, dims, scale, limit, split, heavy, dtype=jnp.bfloat16):
    entries = scale * jax.random.normal(own_key, dims, jnp.float32)
    if split:
        entries = entries * shard_levels(own_key, dims, split, -0.22, 0.18)
    return jnp.clip(spiked(entries, jax.random.fold_in(own_key, 3), *heavy), -limit, limit).astype(dtype)


def setup_inputs(seed: int = 0) -> dict:
    splits = jax.random.split(jax.random.key(seed), 6)
    hidden = gaussian(splits[0], (ISL, TOK, FF), 1.0, 6.0, ((0, 8), (2, 4)))
    island_weights = bell_draw_with(splits[1], (ISL, D, FF), 1.0, 6.0, ((0, 8), (2, 4)), (0, 1, 8, 2.0))
    targets = gaussian(splits[2], (ISL, D, TOK), 1.0, 6.0, ((0, 8), (1, 4)))
    global_weights = gaussian(splits[3], (FRAG, FF), 1.0, 6.0, ((0, 8), (1, 4)), jnp.float32)
    momentum = gaussian(splits[4], (FRAG, FF), 0.4, 3.0, ((0, 8), (1, 4)), jnp.float32)
    return dict(hidden=hidden, island_weights=island_weights, targets=targets, global_weights=global_weights, momentum=momentum)


inner_rate = 0.3
outer_rate = 0.7
outer_beta = 0.9
mix_share = 0.5

def reference(hidden, island_weights, targets, global_weights, momentum):
    scale = 1.0 / math.sqrt(FF)

    def one_island(inputs):
        activations, weights, goals = inputs
        outputs = lax.dot_general(weights, activations, (((1,), (1,)), ((), ())), preferred_element_type=jnp.float32) * scale
        residue = (outputs - goals.astype(jnp.float32)).astype(jnp.bfloat16)
        back = lax.dot_general(residue, weights, (((0,), (0,)), ((), ())), preferred_element_type=jnp.float32) * scale
        grad = jnp.dot(residue[:FRAG], activations, preferred_element_type=jnp.float32) * scale
        return (weights[:FRAG].astype(jnp.float32) - inner_rate * grad, back.astype(jnp.bfloat16))
    inner, grad_hidden = lax.map(one_island, (hidden, island_weights, targets))
    pseudo = global_weights - lax.optimization_barrier(jnp.sum(inner, axis=0)) / ISL
    new_momentum = outer_beta * momentum + pseudo
    new_global = global_weights - outer_rate * (pseudo + outer_beta * new_momentum)
    mixed = (mix_share * inner + (1.0 - mix_share) * new_global[None]).astype(jnp.bfloat16)
    return (mixed, new_global, new_momentum, grad_hidden)
```

```python
import math

import jax
import jax.numpy as jnp
from jax import lax
from jax.experimental import pallas as pl
from jax.experimental.pallas import tpu as pltpu
from jax.sharding import PartitionSpec as P

inner_rate = 0.3
outer_rate = 0.7
outer_beta = 0.9
mix_share = 0.5


VMEM_LIMIT = 54 * 2**20
ANY = pl.BlockSpec(memory_space=pl.ANY)
F32 = jnp.float32
BF16 = jnp.bfloat16


def matmul_nt(a, b):
    return lax.dot_general(a, b, (((1,), (1,)), ((), ())), preferred_element_type=F32)


def add(a, b):
    return (a.astype(F32) + b.astype(F32)).astype(BF16)


def like(x):
    return jax.ShapeDtypeStruct(x.shape, x.dtype)


def options():
    return dict(
        compiler_params=pltpu.CompilerParams(vmem_limit_bytes=VMEM_LIMIT),
        cost_estimate=pl.CostEstimate(flops=1, bytes_accessed=1, transcendentals=0),
    )


def grid_of(grid, ins, outs, scratch=()):
    return pltpu.PrefetchScalarGridSpec(
        num_scalar_prefetch=1, grid=grid, in_specs=ins, out_specs=outs, scratch_shapes=list(scratch)
    )


def swapped(count, bit):
    return [(i, i ^ bit) for i in range(count)]


def across(x, count, bit):
    return lax.ppermute(x, "tensor", swapped(count, bit))


def terms_of(x, count, when=None):
    bit = 4
    while bit < count:
        x = add(x, across(x, count, bit))
        bit *= 2
    terms = [x]
    if count > 2:
        terms.append(across(x, count, 2))
    if when is not None:
        terms = list(join(terms, *when))
    if count > 1:
        terms += [across(term, count, 1) for term in terms]
    return terms


def total_of(values):
    total = values[0].astype(F32)
    for value in values[1:]:
        total += value.astype(F32)
    return total.astype(BF16)


def join(values, *others):
    def kernel(*refs):
        pass

    return pl.pallas_call(
        kernel,
        in_specs=[ANY] * (len(values) + len(others)),
        out_specs=[ANY] * len(values),
        out_shape=[like(x) for x in values],
        input_output_aliases={n: n for n in range(len(values))},
        name="join",
        cost_estimate=pl.CostEstimate(flops=1, bytes_accessed=1, transcendentals=0),
    )(*values, *others)


class Table:
    def __init__(self, pairs, tensor, size, per):
        rows = [r for pair in pairs for r in pair]
        self.count = len(rows)
        self.size = size
        self.values = jnp.stack(
            [lax.div(r, size) for r in rows]
            + [lax.div(lax.rem(r, per), size) for r in rows]
            + [(lax.div(r, per) == tensor).astype(jnp.int32) for r in rows]
            + [tensor]
        )

    def block(self, t, s, n):
        return t[2 * s + n]

    def row(self, t, s, n):
        return pl.multiple_of(t[2 * s + n] * self.size, self.size)

    def goal_row(self, t, s, n):
        return pl.multiple_of(t[self.count + 2 * s + n] * self.size, self.size)

    def goal_here(self, t, s, n):
        return t[2 * self.count + 2 * s + n] == 1

    def tensor(self, t):
        return t[3 * self.count]


def partial_blocks(w, h, goals, first, count, table, scale, when=(), held=()):
    size = table.size
    tokens, width = h.shape
    chunks = next(n for n in (4, 2, 1) if width % (n * 128) == 0)
    span = width // chunks
    blocks = [(first + m, n) for m in range(count) for n in range(2)]
    extra = len(when) + len(held)
    total_rows = len(blocks) * size

    def kernel(t, w_ref, h_ref, *refs):
        g_ref, out = refs[0], refs[1 + extra]
        right, left, goal, w_sem, h_sem, g_sem, o_sem = refs[-7:]

        def goal_copy(at):
            rows = pl.ds(table.goal_row(t, *blocks[at]), size)
            return pltpu.make_async_copy(g_ref.at[rows, :], goal.at[pl.ds(at * size, size), :], g_sem.at[at])

        def copies(c):
            columns = pl.ds(c * span, span)
            yield pltpu.make_async_copy(h_ref.at[:, columns], right.at[:, columns], h_sem.at[c])
            for at, block in enumerate(blocks):
                to = left.at[pl.ds(at * size, size), columns]
                yield pltpu.make_async_copy(w_ref.at[pl.ds(table.row(t, *block), size), columns], to, w_sem.at[c, at])

        for c in range(chunks):
            for copy in copies(c):
                copy.start()
        for at in range(len(blocks)):
            goal_copy(at).start()
        total = None
        for c in range(chunks):
            for copy in copies(c):
                copy.wait()
            columns = pl.ds(c * span, span)
            prod = matmul_nt(left[:, columns], right[:, columns])
            total = prod if total is None else total + prod
        for at, block in enumerate(blocks):
            goal_copy(at).wait()
            rows = pl.ds(at * size, size)
            mine = jnp.where(table.goal_here(t, *block), goal[rows, :].astype(F32), 0.0)
            goal[rows, :] = (total[at * size : (at + 1) * size] * scale - mine).astype(BF16)
        result = pltpu.make_async_copy(goal, out, o_sem)
        result.start()
        result.wait()

    out = pl.pallas_call(
        kernel,
        grid_spec=grid_of(
            (1,),
            [ANY] * (3 + extra),
            [ANY] * (1 + len(held)),
            [
                pltpu.VMEM((tokens, width), BF16),
                pltpu.VMEM((len(blocks) * size, width), BF16),
                pltpu.VMEM((len(blocks) * size, tokens), BF16),
                pltpu.SemaphoreType.DMA((chunks, len(blocks))),
                pltpu.SemaphoreType.DMA((chunks,)),
                pltpu.SemaphoreType.DMA((len(blocks),)),
                pltpu.SemaphoreType.DMA,
            ],
        ),
        out_shape=[jax.ShapeDtypeStruct((total_rows, tokens), BF16)] + [like(x) for x in held],
        input_output_aliases={4 + len(when) + n: 1 + n for n in range(len(held))},
        name="partial_blocks",
        **options(),
    )(table.values, w, h, goals, *when, *held)
    return list(out[:1]), list(out[1:])


def stepped_blocks(w, h, terms, first, count, table, rate, when, split):
    size = table.size
    tokens, width = h.shape
    chunks = next(n for n in (4, 2, 1) if width % (n * 128) == 0)
    span = width // chunks
    blocks = [(first + m, n) for m in range(count) for n in range(2)]
    rows = len(blocks) * size
    parts = 3 if split else 1

    def kernel(t, w_ref, h_ref, *refs):
        t_refs, refs = refs[: len(terms)], refs[len(terms) + len(when) :]
        outs = refs[:parts]
        r_out, right, base, left, more, result, w_sem, h_sem, r_sem, o_sem = refs[parts:]

        def copies(c):
            columns = pl.ds(c * span, span)
            yield pltpu.make_async_copy(h_ref.at[:, columns], right.at[:, columns], h_sem.at[c])
            for at, block in enumerate(blocks):
                to = base.at[pl.ds(at * size, size), columns]
                yield pltpu.make_async_copy(w_ref.at[pl.ds(table.row(t, *block), size), columns], to, w_sem.at[c, at])

        def results(c):
            columns = pl.ds(c * span, span)
            yield pltpu.make_async_copy(result.at[:, columns], outs[0].at[:, columns], o_sem.at[c, 0])
            for n, out in enumerate(outs[1:]):
                part = result.at[pl.ds(n * size, size), columns]
                yield pltpu.make_async_copy(part, out.at[:, columns], o_sem.at[c, 1 + n])

        reads = [pltpu.make_async_copy(ref, more.at[n], r_sem.at[n]) for n, ref in enumerate(t_refs)]
        for copy in reads:
            copy.start()
        for c in range(chunks):
            for copy in copies(c):
                copy.start()
        for copy in reads:
            copy.wait()
        left[...] = total_of([more[n] for n in range(len(terms))])
        keep = pltpu.make_async_copy(left, r_out, r_sem.at[len(terms)])
        keep.start()
        for c in range(chunks):
            for copy in copies(c):
                copy.wait()
            columns = pl.ds(c * span, span)
            step = rate * jnp.dot(left[...], right[:, columns], preferred_element_type=F32)
            result[:, columns] = (base[:, columns].astype(F32) - step).astype(BF16)
            for copy in results(c):
                copy.start()
        for c in range(chunks):
            for copy in results(c):
                copy.wait()
        keep.wait()

    out = pl.pallas_call(
        kernel,
        grid_spec=grid_of(
            (1,),
            [ANY] * (2 + len(terms) + len(when)),
            [ANY] * (parts + 1),
            [
                pltpu.VMEM((tokens, width), BF16),
                pltpu.VMEM((rows, width), BF16),
                pltpu.VMEM((rows, tokens), BF16),
                pltpu.VMEM((len(terms), rows, tokens), BF16),
                pltpu.VMEM((rows, width), BF16),
                pltpu.SemaphoreType.DMA((chunks, len(blocks))),
                pltpu.SemaphoreType.DMA((chunks,)),
                pltpu.SemaphoreType.DMA((len(terms) + 1,)),
                pltpu.SemaphoreType.DMA((chunks, parts)),
            ],
        ),
        out_shape=[jax.ShapeDtypeStruct((rows, width), BF16)]
        + [jax.ShapeDtypeStruct((size, width), BF16)] * (parts - 1)
        + [jax.ShapeDtypeStruct((rows, tokens), BF16)],
        name="stepped_blocks",
        **options(),
    )(table.values, w, h, *terms, *when)
    return list(out[:parts]), out[parts]


def tail_rows(w, h, goals, first, count, tile, table, scale, when, held, blank):
    tokens, width = h.shape
    per = goals.shape[0]
    base = first // tile

    def kernel(t, w_ref, g_ref, h_ref, *refs):
        out, goal = refs[len(when) + len(held)], refs[-1]
        here = lax.div((base + pl.program_id(0)) * tile, per) == table.tensor(t)

        @pl.when(here)
        def _():
            goal[...] = g_ref[...].T

        @pl.when(jnp.logical_not(here))
        def _():
            goal[...] = jnp.zeros_like(goal)

        value = matmul_nt(h_ref[...], w_ref[...]) * scale
        out[...] = (value - goal[...].astype(F32)).astype(BF16)

    out = pl.pallas_call(
        kernel,
        grid_spec=grid_of(
            (count // tile,),
            [
                pl.BlockSpec((tile, width), lambda i, t: (base + i, 0)),
                pl.BlockSpec((tile, tokens), lambda i, t: (lax.rem(base + i, per // tile), 0)),
                pl.BlockSpec((tokens, width), lambda i, t: (0, 0)),
            ]
            + [ANY] * (len(when) + len(held)),
            [pl.BlockSpec((tokens, tile), lambda i, t: (0, i))] + [ANY] * (len(held) + len(blank)),
            [pltpu.VMEM((tokens, tile), BF16)],
        ),
        out_shape=[jax.ShapeDtypeStruct((tokens, count), BF16)]
        + [like(x) for x in held]
        + list(blank),
        input_output_aliases={4 + len(when) + n: 1 + n for n in range(len(held))},
        name="tail_rows",
        **options(),
    )(table.values, w, goals, h, *when, *held)
    return out[0], list(out[1 : 1 + len(held)]), list(out[1 + len(held) :])


def first_features(heads, features, when):
    tokens = heads[0].shape[1]
    frag = sum(x.shape[0] for x in heads)

    def kernel(*refs):
        out, flipped, sem = refs[-3:]
        column = 0
        for ref in refs[: len(heads)]:
            flipped[:, pl.ds(column, ref.shape[0])] = ref[...].T
            column += ref.shape[0]
        copy = pltpu.make_async_copy(flipped, out.at[:, pl.ds(0, frag)], sem)
        copy.start()
        copy.wait()

    return pl.pallas_call(
        kernel,
        grid=(1,),
        in_specs=[pl.BlockSpec(x.shape, lambda i: (0, 0)) for x in heads] + [ANY] * len(when),
        out_specs=ANY,
        out_shape=jax.ShapeDtypeStruct((tokens, features), BF16),
        scratch_shapes=[pltpu.VMEM((tokens, frag), BF16), pltpu.SemaphoreType.DMA],
        name="first_features",
        **options(),
    )(*heads, *when)


def more_features(left, column, terms, when):
    tokens, count = terms[0].shape
    step = count // 2

    def kernel(*refs):
        refs[-1][...] = total_of([ref[...] for ref in refs[: len(terms)]])

    return pl.pallas_call(
        kernel,
        grid=(2,),
        in_specs=[pl.BlockSpec((tokens, step), lambda i: (0, i))] * len(terms) + [ANY] * (1 + len(when)),
        out_specs=pl.BlockSpec((tokens, step), lambda i: (0, column // step + i)),
        out_shape=like(left),
        input_output_aliases={len(terms): 0},
        name="more_features",
        **options(),
    )(*terms, left, *when)


def outer_update(base, moment, total, islands):
    pseudo = base - total / islands
    new_momentum = outer_beta * moment + pseudo
    return base - outer_rate * (pseudo + outer_beta * new_momentum), new_momentum


def outer_step(table, s, got, stored, at, global_weights, momentum, mixed, islands, when):
    size = table.size
    rows, width = global_weights.shape

    steps = next(n for n in (4, 2, 1) if width % (n * 128) == 0)
    span = width // steps

    def kernel(t, a_ref, b_ref, s_ref, g_ref, m_ref, held, *refs):
        g_out, m_out, target, buffer, sems = refs[len(when) :]
        i = pl.program_id(0)

        def copy(i, n):
            part = pl.ds(pl.multiple_of(i * span, span), span)
            to = target.at[pl.ds(table.row(t, s, n), size), part]
            return pltpu.make_async_copy(buffer.at[pl.ds(n * size, size), part], to, sems.at[i, n])

        for n, ref in enumerate((a_ref, b_ref)):
            rows = pl.ds(n * size, size)
            own = s_ref[rows, :].astype(F32)
            new_global, new_momentum = outer_update(g_ref[rows, :], m_ref[rows, :], ref[...].astype(F32) + own, islands)
            g_out[rows, :] = new_global
            m_out[rows, :] = new_momentum
            value = mix_share * own + (1.0 - mix_share) * new_global.astype(BF16).astype(F32)
            buffer[rows, pl.ds(pl.multiple_of(i * span, span), span)] = value.astype(BF16)
            copy(i, n).start()

        @pl.when(i == steps - 1)
        def _():
            for j in range(steps):
                for n in range(2):
                    copy(j, n).wait()

    half = pl.BlockSpec((size, span), lambda i, t: (0, i))
    full = pl.BlockSpec((rows, span), lambda i, t: (0, i))
    return pl.pallas_call(
        kernel,
        grid_spec=grid_of(
            (steps,),
            [half, half, pl.BlockSpec((rows, span), lambda i, t: (at, i)), full, full, ANY] + [ANY] * len(when),
            [full, full, ANY],
            [pltpu.VMEM((rows, width), BF16), pltpu.SemaphoreType.DMA((steps, 2))],
        ),
        out_shape=[like(global_weights), like(momentum), like(mixed)],
        input_output_aliases={6: 2},
        name="outer_step",
        **options(),
    )(table.values, *got, stored, global_weights, momentum, mixed, *when)


def mix_pair(table, s, got, stored, at, mixed):
    size = table.size
    width = mixed.shape[1]

    def kernel(t, a_ref, b_ref, s_ref, held, target, buffer, sems):
        for n, ref in enumerate((a_ref, b_ref)):
            rows = pl.ds(n * size, size)
            value = mix_share * s_ref[rows, :].astype(F32) + (1.0 - mix_share) * ref[...].astype(F32)
            buffer[rows, :] = value.astype(BF16)
        copies = [
            pltpu.make_async_copy(
                buffer.at[pl.ds(n * size, size), :], target.at[pl.ds(table.row(t, s, n), size), :], sems.at[n]
            )
            for n in range(2)
        ]
        for copy in copies:
            copy.start()
        for copy in copies:
            copy.wait()

    return pl.pallas_call(
        kernel,
        grid_spec=grid_of(
            (1,),
            [pl.BlockSpec((size, width), lambda i, t: (0, 0))] * 2
            + [pl.BlockSpec((2 * size, width), lambda i, t: (at, 0)), ANY],
            ANY,
            [pltpu.VMEM((2 * size, width), BF16), pltpu.SemaphoreType.DMA((2,))],
        ),
        out_shape=like(mixed),
        input_output_aliases={4: 0},
        name="mix_pair",
        **options(),
    )(table.values, *got, stored, mixed)


def mix_and_back(w, left, pairs, table, first, count, tile, scale, s, got, stored, at, grad_hidden, mixed):
    size = table.size
    tokens, features = left.shape
    width = w.shape[1]
    blocks = [(m, n) for m in range(pairs) for n in range(2)]
    frag = len(blocks) * size
    more = [mixed] + ([] if grad_hidden is None else [grad_hidden])

    def kernel(t, l_ref, a_ref, b_ref, s_ref, *refs):
        i = pl.program_id(0)
        out, target = refs[len(blocks) + 1 + len(more) : len(blocks) + 3 + len(more)]
        buffer, sems = refs[-2:]

        def copy(n):
            to = target.at[pl.ds(table.row(t, s, n), size), :]
            return pltpu.make_async_copy(buffer.at[pl.ds(n * size, size), :], to, sems.at[n])

        @pl.when(i == 0)
        def _():
            for n, ref in enumerate((a_ref, b_ref)):
                rows = pl.ds(n * size, size)
                value = mix_share * s_ref[rows, :].astype(F32) + (1.0 - mix_share) * ref[...].astype(F32)
                buffer[rows, :] = value.astype(BF16)
                copy(n).start()

        parts = jnp.concatenate([p[...] for p in refs[: len(blocks)]], axis=0)
        total = jnp.dot(l_ref[:, :frag], parts, preferred_element_type=F32)
        total += jnp.dot(l_ref[:, frag:], refs[len(blocks)][...], preferred_element_type=F32)
        out[...] = (total * scale).astype(BF16)

        @pl.when(i == count - 1)
        def _():
            copy(0).wait()
            copy(1).wait()

    operands = 5 + len(blocks) + 1
    aliases = {operands: 1}
    if grad_hidden is not None:
        aliases[operands + 1] = 0

    def block_spec(m, n):
        return pl.BlockSpec((size, tile), lambda i, t: (table.block(t, m, n), first + i))

    rest = pl.BlockSpec((pl.Element(features - frag), pl.Element(tile)), lambda i, t: (frag, (first + i) * tile))
    return pl.pallas_call(
        kernel,
        grid_spec=grid_of(
            (count,),
            [pl.BlockSpec((tokens, features), lambda i, t: (0, 0))]
            + [pl.BlockSpec((size, width), lambda i, t: (0, 0))] * 2
            + [pl.BlockSpec((2 * size, width), lambda i, t: (at, 0))]
            + [block_spec(*x) for x in blocks]
            + [rest]
            + [ANY] * len(more),
            [pl.BlockSpec((tokens, tile), lambda i, t: (0, first + i)), ANY],
            [pltpu.VMEM((2 * size, width), BF16), pltpu.SemaphoreType.DMA((2,))],
        ),
        out_shape=[jax.ShapeDtypeStruct((tokens, width), BF16), like(mixed)],
        input_output_aliases=aliases,
        name="mix_and_back",
        **options(),
    )(table.values, left, *got, stored, *([w] * (len(blocks) + 1)), *more)


def shards(hidden, island_weights, targets, global_weights, momentum):
    h = hidden[0]
    w = island_weights[0]
    goals = targets[0]
    islands = lax.axis_size("island")
    tensors = lax.axis_size("tensor")
    island = lax.axis_index("island")
    tensor = lax.axis_index("tensor")
    rows = global_weights.shape[0]
    size = rows // 2
    frag = rows * islands
    width = w.shape[1]
    scale = 1.0 / math.sqrt(width * tensors)
    rate = inner_rate * scale
    per = goals.shape[0]

    def island_at(k):
        return jnp.where(k < islands // 2, 2 * k, 2 * (islands - 1 - k) + 1)

    def number_at(k):
        return 2 * k if k < islands // 2 else 2 * (islands - 1 - k) + 1

    place = jnp.where(island % 2 == 0, island // 2, islands - 1 - island // 2)
    ahead = [(number_at(k), number_at((k + 1) % islands)) for k in range(islands)]
    back = [(b, a) for a, b in ahead]
    starts = [island_at(lax.rem(place + k, islands)) * rows for k in range(islands)]

    pairs = [(starts[(-s - 1) % islands], starts[(s + 1) % islands] + size) for s in range(islands)]
    table = Table(pairs, tensor, size, per)

    early = 3
    (x,), _ = partial_blocks(w, h, goals, 0, 1, table, scale)
    bit = tensors // 2
    while bit > 1:
        x = add(x, across(x, tensors, bit))
        bit //= 2
    first_terms = [x, across(x, tensors, 1)]
    (x,), _ = partial_blocks(w, h, goals, 1, early, table, scale)
    next_terms = terms_of(x, tensors)
    (first_store, *acc), first_residue = stepped_blocks(w, h, first_terms, 0, 1, table, rate, [], True)

    tile = min(512, per)
    tail_rest = w.shape[0] - frag
    calls = next(n for n in (3, 1) if tail_rest % (n * tile) == 0)
    tail_at = {1: 0, 3: 1, 4: 2}
    tail_due = {5: [0], 6: [1]}
    chips_due = {3: 0, 5: 1}
    tails = []
    mixed = None
    store = {}

    for s in range(islands - 1):
        got = [lax.ppermute(acc[0], "island", ahead), lax.ppermute(acc[1], "island", back)]
        name, at = ("next", s) if s < early else ("last", s - early)
        order = acc
        if s == 0:
            (x,), _ = partial_blocks(w, h, goals, 1 + early, islands - 1 - early, table, scale, order)
            last_terms = terms_of(x, tensors)
            order = [x]
            (store["next"],), next_residue = stepped_blocks(
                w, h, next_terms, 1, early, table, rate, order, False
            )
        if s == early - 1:
            (store["last"],), last_residue = stepped_blocks(
                w, h, last_terms, 1 + early, islands - 1 - early, table, rate, order, False
            )
            order = [last_residue]
        if tail_at.get(s, calls) < calls:
            count = tail_rest // calls
            blank = [jax.ShapeDtypeStruct((frag, width), BF16)] if mixed is None else []
            x, _, fresh = tail_rows(
                w, h, goals, frag + tail_at[s] * count, count, tile, table, scale, order, [], blank
            )
            mixed = fresh[0] if fresh else mixed
            tails.append(terms_of(x, tensors))
            order = [x]
            last_tail = x
        if s == 5:
            left = first_features([first_residue, next_residue, last_residue], w.shape[0], order)
            order = [left]
        for n in tail_due.get(s, []):
            left = more_features(left, frag + n * tails[n][0].shape[1], tails[n], [] if s == 5 else order)
            order = [left]
        if order is not acc and s > 0:
            due = [tails[chips_due[s]][1]] if chips_due.get(s, len(tails)) < len(tails) else []
            (store[name],) = join([store[name]], *order, *due)
        own = [lax.slice_in_dim(store[name], (2 * at + n) * size, (2 * at + n + 1) * size, axis=0) for n in range(2)]
        if s < islands - 2:
            acc = [add(got[i], own[i]) for i in range(2)]
    send = []
    for n in range(2):
        base, moment = (lax.slice_in_dim(x, n * size, (n + 1) * size, axis=0) for x in (global_weights, momentum))
        send.append(outer_update(base, moment, got[n].astype(F32) + own[n].astype(F32), islands)[0].astype(BF16))

    def stored(s):
        if s == 0:
            return first_store, 0
        return (store["next"], s - 1) if s <= early else (store["last"], s - 1 - early)

    wide = 256 if width % 256 == 0 else 128
    tiles = width // wide
    pieces = min(5, tiles, islands - 3)
    cuts = [-(-tiles * n // pieces) for n in range(pieces + 1)]
    grad_hidden = None

    new_global, new_momentum, mixed = outer_step(
        table, islands - 1, got, *stored(islands - 1), global_weights, momentum, mixed, islands, send
    )
    later = range(sum(len(x) for x in tail_due.values()), len(tails))
    waiting = []
    for s in range(islands - 1):
        send = [lax.ppermute(send[0], "island", ahead), lax.ppermute(send[1], "island", back)]
        if s == 0:
            send = join(send, mixed)
        if waiting:
            send = join(send, *waiting)
        piece = s - (islands - 2 - pieces)
        if 0 <= piece < pieces:
            grad_hidden, mixed = mix_and_back(
                w, left, islands, table, cuts[piece], cuts[piece + 1] - cuts[piece], wide, scale, s, send, *stored(s),
                grad_hidden, mixed,
            )
            waiting = [mixed]
        else:
            mixed = mix_pair(table, s, send, *stored(s), mixed)
        if s == 0 and later:
            terms = terms_of(last_tail, tensors, send)
            for n in later:
                left = more_features(left, frag + n * terms[0].shape[1], terms, [mixed])
            waiting = [mixed, left]
    return (mixed[None], new_global, new_momentum, grad_hidden[None])


def solution(mesh):
    return jax.shard_map(
        shards,
        mesh=mesh,
        in_specs=(
            P("island", None, "tensor"),
            P("island", None, "tensor"),
            P("island", "tensor", None),
            P("island", "tensor"),
            P("island", "tensor"),
        ),
        out_specs=(
            P("island", None, "tensor"),
            P("island", "tensor"),
            P("island", "tensor"),
            P("island", None, "tensor"),
        ),
        check_vma=False,
    )
```

```python
import math

import jax
import jax.numpy as jnp
from jax import lax
from jax.experimental import pallas as pl
from jax.experimental.pallas import tpu as pltpu
from jax.sharding import PartitionSpec as P

inner_rate = 0.3
outer_rate = 0.7
outer_beta = 0.9
mix_share = 0.5


MIB = 2**20
ANY = pl.BlockSpec(memory_space=pl.ANY)
F32 = jnp.float32
BF16 = jnp.bfloat16


def matmul_nt(a, b):
    return lax.dot_general(a, b, (((1,), (1,)), ((), ())), preferred_element_type=F32)


def add(a, b):
    return (a.astype(F32) + b.astype(F32)).astype(BF16)


def like(x):
    return jax.ShapeDtypeStruct(x.shape, x.dtype)


def options(limit=50):
    return dict(
        compiler_params=pltpu.CompilerParams(vmem_limit_bytes=limit * MIB),
        cost_estimate=pl.CostEstimate(flops=1, bytes_accessed=1, transcendentals=0),
    )


def grid_of(grid, ins, outs, scratch=()):
    return pltpu.PrefetchScalarGridSpec(
        num_scalar_prefetch=1, grid=grid, in_specs=ins, out_specs=outs, scratch_shapes=list(scratch)
    )


def swapped(count, bit):
    return [(i, i ^ bit) for i in range(count)]


def across(x, count, bit):
    return lax.ppermute(x, "tensor", swapped(count, bit))


def terms_of(x, count, when=None):
    bit = 4
    while bit < count:
        x = add(x, across(x, count, bit))
        bit *= 2
    terms = [x]
    if count > 2:
        terms.append(across(x, count, 2))
    if when is not None:
        terms = list(join(terms, *when))
    if count > 1:
        terms += [across(term, count, 1) for term in terms]
    return terms


def total_of(values):
    total = values[0].astype(F32)
    for value in values[1:]:
        total += value.astype(F32)
    return total.astype(BF16)


def join(values, *others):
    def kernel(*refs):
        pass

    return pl.pallas_call(
        kernel,
        in_specs=[ANY] * (len(values) + len(others)),
        out_specs=[ANY] * len(values),
        out_shape=[like(x) for x in values],
        input_output_aliases={n: n for n in range(len(values))},
        name="join",
        cost_estimate=pl.CostEstimate(flops=1, bytes_accessed=1, transcendentals=0),
    )(*values, *others)


class Table:
    def __init__(self, pairs, tensor, size, per):
        rows = [r for pair in pairs for r in pair]
        self.count = len(rows)
        self.size = size
        self.values = jnp.stack(
            [lax.div(r, size) for r in rows]
            + [lax.div(lax.rem(r, per), size) for r in rows]
            + [(lax.div(r, per) == tensor).astype(jnp.int32) for r in rows]
            + [tensor]
        )

    def block(self, t, s, n):
        return t[2 * s + n]

    def row(self, t, s, n):
        return pl.multiple_of(t[2 * s + n] * self.size, self.size)

    def goal_row(self, t, s, n):
        return pl.multiple_of(t[self.count + 2 * s + n] * self.size, self.size)

    def goal_here(self, t, s, n):
        return t[2 * self.count + 2 * s + n] == 1

    def tensor(self, t):
        return t[3 * self.count]


def partial_blocks(w, h, goals, first, count, table, scale, when=(), held=()):
    size = table.size
    tokens, width = h.shape
    chunks = next(n for n in (4, 2, 1) if width % (n * 128) == 0)
    span = width // chunks
    blocks = [(first + m, n) for m in range(count) for n in range(2)]
    extra = len(when) + len(held)
    total_rows = len(blocks) * size

    def kernel(t, w_ref, h_ref, *refs):
        g_ref, out = refs[0], refs[1 + extra]
        right, left, goal, w_sem, h_sem, g_sem, o_sem = refs[-7:]

        def goal_copy(at):
            rows = pl.ds(table.goal_row(t, *blocks[at]), size)
            return pltpu.make_async_copy(g_ref.at[rows, :], goal.at[pl.ds(at * size, size), :], g_sem.at[at])

        def copies(c):
            columns = pl.ds(c * span, span)
            yield pltpu.make_async_copy(h_ref.at[:, columns], right.at[:, columns], h_sem.at[c])
            for at, block in enumerate(blocks):
                to = left.at[pl.ds(at * size, size), columns]
                yield pltpu.make_async_copy(w_ref.at[pl.ds(table.row(t, *block), size), columns], to, w_sem.at[c, at])

        for c in range(chunks):
            for copy in copies(c):
                copy.start()
        for at in range(len(blocks)):
            goal_copy(at).start()
        total = None
        for c in range(chunks):
            for copy in copies(c):
                copy.wait()
            columns = pl.ds(c * span, span)
            prod = matmul_nt(left[:, columns], right[:, columns])
            total = prod if total is None else total + prod
        for at, block in enumerate(blocks):
            goal_copy(at).wait()
            rows = pl.ds(at * size, size)
            mine = jnp.where(table.goal_here(t, *block), goal[rows, :].astype(F32), 0.0)
            goal[rows, :] = (total[at * size : (at + 1) * size] * scale - mine).astype(BF16)
        result = pltpu.make_async_copy(goal, out, o_sem)
        result.start()
        result.wait()

    out = pl.pallas_call(
        kernel,
        grid_spec=grid_of(
            (1,),
            [ANY] * (3 + extra),
            [ANY] * (1 + len(held)),
            [
                pltpu.VMEM((tokens, width), BF16),
                pltpu.VMEM((len(blocks) * size, width), BF16),
                pltpu.VMEM((len(blocks) * size, tokens), BF16),
                pltpu.SemaphoreType.DMA((chunks, len(blocks))),
                pltpu.SemaphoreType.DMA((chunks,)),
                pltpu.SemaphoreType.DMA((len(blocks),)),
                pltpu.SemaphoreType.DMA,
            ],
        ),
        out_shape=[jax.ShapeDtypeStruct((total_rows, tokens), BF16)] + [like(x) for x in held],
        input_output_aliases={4 + len(when) + n: 1 + n for n in range(len(held))},
        name="partial_blocks",
        **options(),
    )(table.values, w, h, goals, *when, *held)
    return list(out[:1]), list(out[1:])


def stepped_blocks(w, h, terms, first, count, table, rate, when, split):
    size = table.size
    tokens, width = h.shape
    chunks = next(n for n in (4, 2, 1) if width % (n * 128) == 0)
    span = width // chunks
    blocks = [(first + m, n) for m in range(count) for n in range(2)]
    rows = len(blocks) * size
    parts = 3 if split else 1

    def kernel(t, w_ref, h_ref, *refs):
        t_refs, refs = refs[: len(terms)], refs[len(terms) + len(when) :]
        outs = refs[:parts]
        r_out, right, base, left, more, result, w_sem, h_sem, r_sem, o_sem = refs[parts:]

        def copies(c):
            columns = pl.ds(c * span, span)
            yield pltpu.make_async_copy(h_ref.at[:, columns], right.at[:, columns], h_sem.at[c])
            for at, block in enumerate(blocks):
                to = base.at[pl.ds(at * size, size), columns]
                yield pltpu.make_async_copy(w_ref.at[pl.ds(table.row(t, *block), size), columns], to, w_sem.at[c, at])

        def results(c):
            columns = pl.ds(c * span, span)
            yield pltpu.make_async_copy(result.at[:, columns], outs[0].at[:, columns], o_sem.at[c, 0])
            for n, out in enumerate(outs[1:]):
                part = result.at[pl.ds(n * size, size), columns]
                yield pltpu.make_async_copy(part, out.at[:, columns], o_sem.at[c, 1 + n])

        reads = [pltpu.make_async_copy(ref, more.at[n], r_sem.at[n]) for n, ref in enumerate(t_refs)]
        for copy in reads:
            copy.start()
        for c in range(chunks):
            for copy in copies(c):
                copy.start()
        for copy in reads:
            copy.wait()
        left[...] = total_of([more[n] for n in range(len(terms))])
        keep = pltpu.make_async_copy(left, r_out, r_sem.at[len(terms)])
        keep.start()
        for c in range(chunks):
            for copy in copies(c):
                copy.wait()
            columns = pl.ds(c * span, span)
            step = rate * jnp.dot(left[...], right[:, columns], preferred_element_type=F32)
            result[:, columns] = (base[:, columns].astype(F32) - step).astype(BF16)
            for copy in results(c):
                copy.start()
        for c in range(chunks):
            for copy in results(c):
                copy.wait()
        keep.wait()

    out = pl.pallas_call(
        kernel,
        grid_spec=grid_of(
            (1,),
            [ANY] * (2 + len(terms) + len(when)),
            [ANY] * (parts + 1),
            [
                pltpu.VMEM((tokens, width), BF16),
                pltpu.VMEM((rows, width), BF16),
                pltpu.VMEM((rows, tokens), BF16),
                pltpu.VMEM((len(terms), rows, tokens), BF16),
                pltpu.VMEM((rows, width), BF16),
                pltpu.SemaphoreType.DMA((chunks, len(blocks))),
                pltpu.SemaphoreType.DMA((chunks,)),
                pltpu.SemaphoreType.DMA((len(terms) + 1,)),
                pltpu.SemaphoreType.DMA((chunks, parts)),
            ],
        ),
        out_shape=[jax.ShapeDtypeStruct((rows, width), BF16)]
        + [jax.ShapeDtypeStruct((size, width), BF16)] * (parts - 1)
        + [jax.ShapeDtypeStruct((rows, tokens), BF16)],
        name="stepped_blocks",
        **options(),
    )(table.values, w, h, *terms, *when)
    return list(out[:parts]), out[parts]


def tail_rows(w, h, goals, first, count, tile, table, scale, when, held, blank):
    tokens, width = h.shape
    per = goals.shape[0]
    base = first // tile

    def kernel(t, w_ref, g_ref, h_ref, *refs):
        out, goal = refs[len(when) + len(held)], refs[-1]
        here = lax.div((base + pl.program_id(0)) * tile, per) == table.tensor(t)

        @pl.when(here)
        def _():
            goal[...] = g_ref[...].T

        @pl.when(jnp.logical_not(here))
        def _():
            goal[...] = jnp.zeros_like(goal)

        value = matmul_nt(h_ref[...], w_ref[...]) * scale
        out[...] = (value - goal[...].astype(F32)).astype(BF16)

    out = pl.pallas_call(
        kernel,
        grid_spec=grid_of(
            (count // tile,),
            [
                pl.BlockSpec((tile, width), lambda i, t: (base + i, 0)),
                pl.BlockSpec((tile, tokens), lambda i, t: (lax.rem(base + i, per // tile), 0)),
                pl.BlockSpec((tokens, width), lambda i, t: (0, 0)),
            ]
            + [ANY] * (len(when) + len(held)),
            [pl.BlockSpec((tokens, tile), lambda i, t: (0, i))] + [ANY] * (len(held) + len(blank)),
            [pltpu.VMEM((tokens, tile), BF16)],
        ),
        out_shape=[jax.ShapeDtypeStruct((tokens, count), BF16)]
        + [like(x) for x in held]
        + list(blank),
        input_output_aliases={4 + len(when) + n: 1 + n for n in range(len(held))},
        name="tail_rows",
        **options(),
    )(table.values, w, goals, h, *when, *held)
    return out[0], list(out[1 : 1 + len(held)]), list(out[1 + len(held) :])


def first_features(heads, features, when):
    tokens = heads[0].shape[1]
    frag = sum(x.shape[0] for x in heads)

    def kernel(*refs):
        out, flipped, sem = refs[-3:]
        column = 0
        for ref in refs[: len(heads)]:
            flipped[:, pl.ds(column, ref.shape[0])] = ref[...].T
            column += ref.shape[0]
        copy = pltpu.make_async_copy(flipped, out.at[:, pl.ds(0, frag)], sem)
        copy.start()
        copy.wait()

    return pl.pallas_call(
        kernel,
        grid=(1,),
        in_specs=[pl.BlockSpec(x.shape, lambda i: (0, 0)) for x in heads] + [ANY] * len(when),
        out_specs=ANY,
        out_shape=jax.ShapeDtypeStruct((tokens, features), BF16),
        scratch_shapes=[pltpu.VMEM((tokens, frag), BF16), pltpu.SemaphoreType.DMA],
        name="first_features",
        **options(),
    )(*heads, *when)


def more_features(left, column, terms, when):
    tokens, count = terms[0].shape
    step = count // 2

    def kernel(*refs):
        refs[-1][...] = total_of([ref[...] for ref in refs[: len(terms)]])

    return pl.pallas_call(
        kernel,
        grid=(2,),
        in_specs=[pl.BlockSpec((tokens, step), lambda i: (0, i))] * len(terms) + [ANY] * (1 + len(when)),
        out_specs=pl.BlockSpec((tokens, step), lambda i: (0, column // step + i)),
        out_shape=like(left),
        input_output_aliases={len(terms): 0},
        name="more_features",
        **options(),
    )(*terms, left, *when)


def outer_update(base, moment, total, islands):
    pseudo = base - total / islands
    new_momentum = outer_beta * moment + pseudo
    return base - outer_rate * (pseudo + outer_beta * new_momentum), new_momentum


def outer_step(table, s, got, stored, at, global_weights, momentum, mixed, islands, when):
    size = table.size
    rows, width = global_weights.shape

    steps = next(n for n in (4, 2, 1) if width % (n * 128) == 0)
    span = width // steps

    def kernel(t, a_ref, b_ref, s_ref, g_ref, m_ref, held, *refs):
        g_out, m_out, target, buffer, sems = refs[len(when) :]
        i = pl.program_id(0)

        def copy(i, n):
            part = pl.ds(pl.multiple_of(i * span, span), span)
            to = target.at[pl.ds(table.row(t, s, n), size), part]
            return pltpu.make_async_copy(buffer.at[pl.ds(n * size, size), part], to, sems.at[i, n])

        for n, ref in enumerate((a_ref, b_ref)):
            rows = pl.ds(n * size, size)
            own = s_ref[rows, :].astype(F32)
            new_global, new_momentum = outer_update(g_ref[rows, :], m_ref[rows, :], ref[...].astype(F32) + own, islands)
            g_out[rows, :] = new_global
            m_out[rows, :] = new_momentum
            value = mix_share * own + (1.0 - mix_share) * new_global.astype(BF16).astype(F32)
            buffer[rows, pl.ds(pl.multiple_of(i * span, span), span)] = value.astype(BF16)
            copy(i, n).start()

        @pl.when(i == steps - 1)
        def _():
            for j in range(steps):
                for n in range(2):
                    copy(j, n).wait()

    half = pl.BlockSpec((size, span), lambda i, t: (0, i))
    full = pl.BlockSpec((rows, span), lambda i, t: (0, i))
    return pl.pallas_call(
        kernel,
        grid_spec=grid_of(
            (steps,),
            [half, half, pl.BlockSpec((rows, span), lambda i, t: (at, i)), full, full, ANY] + [ANY] * len(when),
            [full, full, ANY],
            [pltpu.VMEM((rows, width), BF16), pltpu.SemaphoreType.DMA((steps, 2))],
        ),
        out_shape=[like(global_weights), like(momentum), like(mixed)],
        input_output_aliases={6: 2},
        name="outer_step",
        **options(),
    )(table.values, *got, stored, global_weights, momentum, mixed, *when)


def mix_pair(table, s, got, stored, at, mixed):
    size = table.size
    width = mixed.shape[1]

    def kernel(t, a_ref, b_ref, s_ref, held, target, buffer, sems):
        for n, ref in enumerate((a_ref, b_ref)):
            rows = pl.ds(n * size, size)
            value = mix_share * s_ref[rows, :].astype(F32) + (1.0 - mix_share) * ref[...].astype(F32)
            buffer[rows, :] = value.astype(BF16)
        copies = [
            pltpu.make_async_copy(
                buffer.at[pl.ds(n * size, size), :], target.at[pl.ds(table.row(t, s, n), size), :], sems.at[n]
            )
            for n in range(2)
        ]
        for copy in copies:
            copy.start()
        for copy in copies:
            copy.wait()

    return pl.pallas_call(
        kernel,
        grid_spec=grid_of(
            (1,),
            [pl.BlockSpec((size, width), lambda i, t: (0, 0))] * 2
            + [pl.BlockSpec((2 * size, width), lambda i, t: (at, 0)), ANY],
            ANY,
            [pltpu.VMEM((2 * size, width), BF16), pltpu.SemaphoreType.DMA((2,))],
        ),
        out_shape=like(mixed),
        input_output_aliases={4: 0},
        name="mix_pair",
        **options(58),
    )(table.values, *got, stored, mixed)


def mix_and_back(w, left, pairs, table, first, count, tile, scale, s, got, stored, at, grad_hidden, mixed):
    size = table.size
    tokens, features = left.shape
    width = w.shape[1]
    blocks = [(m, n) for m in range(pairs) for n in range(2)]
    frag = len(blocks) * size
    more = [mixed] + ([] if grad_hidden is None else [grad_hidden])

    def kernel(t, l_ref, a_ref, b_ref, s_ref, *refs):
        i = pl.program_id(0)
        out, target = refs[len(blocks) + 1 + len(more) : len(blocks) + 3 + len(more)]
        buffer, sems = refs[-2:]

        def copy(n):
            to = target.at[pl.ds(table.row(t, s, n), size), :]
            return pltpu.make_async_copy(buffer.at[pl.ds(n * size, size), :], to, sems.at[n])

        @pl.when(i == 0)
        def _():
            for n, ref in enumerate((a_ref, b_ref)):
                rows = pl.ds(n * size, size)
                value = mix_share * s_ref[rows, :].astype(F32) + (1.0 - mix_share) * ref[...].astype(F32)
                buffer[rows, :] = value.astype(BF16)
                copy(n).start()

        parts = jnp.concatenate([p[...] for p in refs[: len(blocks)]], axis=0)
        total = jnp.dot(l_ref[:, :frag], parts, preferred_element_type=F32)
        total += jnp.dot(l_ref[:, frag:], refs[len(blocks)][...], preferred_element_type=F32)
        out[...] = (total * scale).astype(BF16)

        @pl.when(i == count - 1)
        def _():
            copy(0).wait()
            copy(1).wait()

    operands = 5 + len(blocks) + 1
    aliases = {operands: 1}
    if grad_hidden is not None:
        aliases[operands + 1] = 0

    def block_spec(m, n):
        return pl.BlockSpec((size, tile), lambda i, t: (table.block(t, m, n), first + i))

    rest = pl.BlockSpec((pl.Element(features - frag), pl.Element(tile)), lambda i, t: (frag, (first + i) * tile))
    return pl.pallas_call(
        kernel,
        grid_spec=grid_of(
            (count,),
            [pl.BlockSpec((tokens, features), lambda i, t: (0, 0))]
            + [pl.BlockSpec((size, width), lambda i, t: (0, 0))] * 2
            + [pl.BlockSpec((2 * size, width), lambda i, t: (at, 0))]
            + [block_spec(*x) for x in blocks]
            + [rest]
            + [ANY] * len(more),
            [pl.BlockSpec((tokens, tile), lambda i, t: (0, first + i)), ANY],
            [pltpu.VMEM((2 * size, width), BF16), pltpu.SemaphoreType.DMA((2,))],
        ),
        out_shape=[jax.ShapeDtypeStruct((tokens, width), BF16), like(mixed)],
        input_output_aliases=aliases,
        name="mix_and_back",
        **options(58),
    )(table.values, left, *got, stored, *([w] * (len(blocks) + 1)), *more)


def shards(hidden, island_weights, targets, global_weights, momentum):
    h = hidden[0]
    w = island_weights[0]
    goals = targets[0]
    islands = lax.axis_size("island")
    tensors = lax.axis_size("tensor")
    island = lax.axis_index("island")
    tensor = lax.axis_index("tensor")
    rows = global_weights.shape[0]
    size = rows // 2
    frag = rows * islands
    width = w.shape[1]
    scale = 1.0 / math.sqrt(width * tensors)
    rate = inner_rate * scale
    per = goals.shape[0]

    def island_at(k):
        return jnp.where(k < islands // 2, 2 * k, 2 * (islands - 1 - k) + 1)

    def number_at(k):
        return 2 * k if k < islands // 2 else 2 * (islands - 1 - k) + 1

    place = jnp.where(island % 2 == 0, island // 2, islands - 1 - island // 2)
    ahead = [(number_at(k), number_at((k + 1) % islands)) for k in range(islands)]
    back = [(b, a) for a, b in ahead]
    starts = [island_at(lax.rem(place + k, islands)) * rows for k in range(islands)]

    pairs = [(starts[(-s - 1) % islands], starts[(s + 1) % islands] + size) for s in range(islands)]
    table = Table(pairs, tensor, size, per)

    early = 3
    (x,), _ = partial_blocks(w, h, goals, 0, 1, table, scale)
    bit = tensors // 2
    while bit > 1:
        x = add(x, across(x, tensors, bit))
        bit //= 2
    first_terms = [x, across(x, tensors, 1)]
    (x,), _ = partial_blocks(w, h, goals, 1, early, table, scale)
    next_terms = terms_of(x, tensors)
    (first_store, *acc), first_residue = stepped_blocks(w, h, first_terms, 0, 1, table, rate, [], True)

    tile = min(512, per)
    tail_rest = w.shape[0] - frag
    calls = next(n for n in (3, 1) if tail_rest % (n * tile) == 0)
    tail_at = {1: 0, 3: 1, 4: 2}
    tail_due = {5: [0], 6: [1]}
    chips_due = {3: 0, 5: 1}
    tails = []
    mixed = None
    store = {}

    for s in range(islands - 1):
        got = [lax.ppermute(acc[0], "island", ahead), lax.ppermute(acc[1], "island", back)]
        name, at = ("next", s) if s < early else ("last", s - early)
        order = acc
        if s == 0:
            (x,), _ = partial_blocks(w, h, goals, 1 + early, islands - 1 - early, table, scale, order)
            last_terms = terms_of(x, tensors)
            order = [x]
            (store["next"],), next_residue = stepped_blocks(
                w, h, next_terms, 1, early, table, rate, order, False
            )
        if s == early - 1:
            (store["last"],), last_residue = stepped_blocks(
                w, h, last_terms, 1 + early, islands - 1 - early, table, rate, order, False
            )
            order = [last_residue]
        if tail_at.get(s, calls) < calls:
            count = tail_rest // calls
            blank = [jax.ShapeDtypeStruct((frag, width), BF16)] if mixed is None else []
            x, _, fresh = tail_rows(
                w, h, goals, frag + tail_at[s] * count, count, tile, table, scale, order, [], blank
            )
            mixed = fresh[0] if fresh else mixed
            tails.append(terms_of(x, tensors))
            order = [x]
            last_tail = x
        if s == 5:
            left = first_features([first_residue, next_residue, last_residue], w.shape[0], order)
            order = [left]
        for n in tail_due.get(s, []):
            left = more_features(left, frag + n * tails[n][0].shape[1], tails[n], [] if s == 5 else order)
            order = [left]
        if order is not acc and s > 0:
            due = [tails[chips_due[s]][1]] if chips_due.get(s, len(tails)) < len(tails) else []
            (store[name],) = join([store[name]], *order, *due)
        own = [lax.slice_in_dim(store[name], (2 * at + n) * size, (2 * at + n + 1) * size, axis=0) for n in range(2)]
        if s < islands - 2:
            acc = [add(got[i], own[i]) for i in range(2)]
    send = []
    for n in range(2):
        base, moment = (lax.slice_in_dim(x, n * size, (n + 1) * size, axis=0) for x in (global_weights, momentum))
        send.append(outer_update(base, moment, got[n].astype(F32) + own[n].astype(F32), islands)[0].astype(BF16))

    def stored(s):
        if s == 0:
            return first_store, 0
        return (store["next"], s - 1) if s <= early else (store["last"], s - 1 - early)

    wide = 256 if width % 256 == 0 else 128
    tiles = width // wide
    pieces = min(5, tiles, islands - 3)
    cuts = [-(-tiles * n // pieces) for n in range(pieces + 1)]
    grad_hidden = None

    new_global, new_momentum, mixed = outer_step(
        table, islands - 1, got, *stored(islands - 1), global_weights, momentum, mixed, islands, send
    )
    later = range(sum(len(x) for x in tail_due.values()), len(tails))
    waiting = []
    for s in range(islands - 1):
        send = [lax.ppermute(send[0], "island", ahead), lax.ppermute(send[1], "island", back)]
        if s == 0:
            send = join(send, mixed)
        if waiting:
            send = join(send, *waiting)
        piece = s - (islands - 2 - pieces)
        if 0 <= piece < pieces:
            grad_hidden, mixed = mix_and_back(
                w, left, islands, table, cuts[piece], cuts[piece + 1] - cuts[piece], wide, scale, s, send, *stored(s),
                grad_hidden, mixed,
            )
            waiting = [mixed]
        else:
            mixed = mix_pair(table, s, send, *stored(s), mixed)
        if s == 0 and later:
            terms = terms_of(last_tail, tensors, send)
            for n in later:
                left = more_features(left, frag + n * terms[0].shape[1], terms, [mixed])
            waiting = [mixed, left]
    return (mixed[None], new_global, new_momentum, grad_hidden[None])


def solution(mesh):
    return jax.shard_map(
        shards,
        mesh=mesh,
        in_specs=(
            P("island", None, "tensor"),
            P("island", None, "tensor"),
            P("island", "tensor", None),
            P("island", "tensor"),
            P("island", "tensor"),
        ),
        out_specs=(
            P("island", None, "tensor"),
            P("island", "tensor"),
            P("island", "tensor"),
            P("island", None, "tensor"),
        ),
        check_vma=False,
    )
```

```python
import math

import jax
import jax.numpy as jnp
from jax import lax
from jax.experimental import pallas as pl
from jax.experimental.pallas import tpu as pltpu
from jax.sharding import PartitionSpec as P

inner_rate = 0.3
outer_rate = 0.7
outer_beta = 0.9
mix_share = 0.5


MIB = 2**20
ANY = pl.BlockSpec(memory_space=pl.ANY)
F32 = jnp.float32
BF16 = jnp.bfloat16


def matmul_nt(a, b):
    return lax.dot_general(a, b, (((1,), (1,)), ((), ())), preferred_element_type=F32)


def add(a, b):
    return (a.astype(F32) + b.astype(F32)).astype(BF16)


def like(x):
    return jax.ShapeDtypeStruct(x.shape, x.dtype)


def options(limit=50):
    return dict(
        compiler_params=pltpu.CompilerParams(vmem_limit_bytes=limit * MIB),
        cost_estimate=pl.CostEstimate(flops=1, bytes_accessed=1, transcendentals=0),
    )


def grid_of(grid, ins, outs, scratch=()):
    return pltpu.PrefetchScalarGridSpec(
        num_scalar_prefetch=1, grid=grid, in_specs=ins, out_specs=outs, scratch_shapes=list(scratch)
    )


def swapped(count, bit):
    return [(i, i ^ bit) for i in range(count)]


def across(x, count, bit):
    return lax.ppermute(x, "tensor", swapped(count, bit))


def terms_of(x, count, when=None):
    bit = 4
    while bit < count:
        x = add(x, across(x, count, bit))
        bit *= 2
    terms = [x]
    if count > 2:
        terms.append(across(x, count, 2))
    if when is not None:
        terms = list(join(terms, *when))
    if count > 1:
        terms += [across(term, count, 1) for term in terms]
    return terms


def total_of(values):
    total = values[0].astype(F32)
    for value in values[1:]:
        total += value.astype(F32)
    return total.astype(BF16)


def join(values, *others):
    def kernel(*refs):
        pass

    return pl.pallas_call(
        kernel,
        in_specs=[ANY] * (len(values) + len(others)),
        out_specs=[ANY] * len(values),
        out_shape=[like(x) for x in values],
        input_output_aliases={n: n for n in range(len(values))},
        name="join",
        cost_estimate=pl.CostEstimate(flops=1, bytes_accessed=1, transcendentals=0),
    )(*values, *others)


class Table:
    def __init__(self, pairs, tensor, size, per):
        rows = [r for pair in pairs for r in pair]
        self.count = len(rows)
        self.size = size
        self.values = jnp.stack(
            [lax.div(r, size) for r in rows]
            + [lax.div(lax.rem(r, per), size) for r in rows]
            + [(lax.div(r, per) == tensor).astype(jnp.int32) for r in rows]
            + [tensor]
        )

    def block(self, t, s, n):
        return t[2 * s + n]

    def row(self, t, s, n):
        return pl.multiple_of(t[2 * s + n] * self.size, self.size)

    def goal_row(self, t, s, n):
        return pl.multiple_of(t[self.count + 2 * s + n] * self.size, self.size)

    def goal_here(self, t, s, n):
        return t[2 * self.count + 2 * s + n] == 1

    def tensor(self, t):
        return t[3 * self.count]


def partial_blocks(w, h, goals, first, count, table, scale, when=(), held=()):
    size = table.size
    tokens, width = h.shape
    chunks = next(n for n in (4, 2, 1) if width % (n * 128) == 0)
    span = width // chunks
    blocks = [(first + m, n) for m in range(count) for n in range(2)]
    extra = len(when) + len(held)
    total_rows = len(blocks) * size

    def kernel(t, w_ref, h_ref, *refs):
        g_ref, out = refs[0], refs[1 + extra]
        right, left, goal, w_sem, h_sem, g_sem, o_sem = refs[-7:]

        def goal_copy(at):
            rows = pl.ds(table.goal_row(t, *blocks[at]), size)
            return pltpu.make_async_copy(g_ref.at[rows, :], goal.at[pl.ds(at * size, size), :], g_sem.at[at])

        def copies(c):
            columns = pl.ds(c * span, span)
            yield pltpu.make_async_copy(h_ref.at[:, columns], right.at[:, columns], h_sem.at[c])
            for at, block in enumerate(blocks):
                to = left.at[pl.ds(at * size, size), columns]
                yield pltpu.make_async_copy(w_ref.at[pl.ds(table.row(t, *block), size), columns], to, w_sem.at[c, at])

        for c in range(chunks):
            for copy in copies(c):
                copy.start()
        for at in range(len(blocks)):
            goal_copy(at).start()
        total = None
        for c in range(chunks):
            for copy in copies(c):
                copy.wait()
            columns = pl.ds(c * span, span)
            prod = matmul_nt(left[:, columns], right[:, columns])
            total = prod if total is None else total + prod
        for at, block in enumerate(blocks):
            goal_copy(at).wait()
            rows = pl.ds(at * size, size)
            mine = jnp.where(table.goal_here(t, *block), goal[rows, :].astype(F32), 0.0)
            goal[rows, :] = (total[at * size : (at + 1) * size] * scale - mine).astype(BF16)
        result = pltpu.make_async_copy(goal, out, o_sem)
        result.start()
        result.wait()

    out = pl.pallas_call(
        kernel,
        grid_spec=grid_of(
            (1,),
            [ANY] * (3 + extra),
            [ANY] * (1 + len(held)),
            [
                pltpu.VMEM((tokens, width), BF16),
                pltpu.VMEM((len(blocks) * size, width), BF16),
                pltpu.VMEM((len(blocks) * size, tokens), BF16),
                pltpu.SemaphoreType.DMA((chunks, len(blocks))),
                pltpu.SemaphoreType.DMA((chunks,)),
                pltpu.SemaphoreType.DMA((len(blocks),)),
                pltpu.SemaphoreType.DMA,
            ],
        ),
        out_shape=[jax.ShapeDtypeStruct((total_rows, tokens), BF16)] + [like(x) for x in held],
        input_output_aliases={4 + len(when) + n: 1 + n for n in range(len(held))},
        name="partial_blocks",
        **options(),
    )(table.values, w, h, goals, *when, *held)
    return list(out[:1]), list(out[1:])


def stepped_blocks(w, h, terms, first, count, table, rate, when, split):
    size = table.size
    tokens, width = h.shape
    chunks = next(n for n in (4, 2, 1) if width % (n * 128) == 0)
    span = width // chunks
    blocks = [(first + m, n) for m in range(count) for n in range(2)]
    rows = len(blocks) * size
    parts = 3 if split else 1

    def kernel(t, w_ref, h_ref, *refs):
        t_refs, refs = refs[: len(terms)], refs[len(terms) + len(when) :]
        outs = refs[:parts]
        r_out, right, base, left, more, result, w_sem, h_sem, r_sem, o_sem = refs[parts:]

        def copies(c):
            columns = pl.ds(c * span, span)
            yield pltpu.make_async_copy(h_ref.at[:, columns], right.at[:, columns], h_sem.at[c])
            for at, block in enumerate(blocks):
                to = base.at[pl.ds(at * size, size), columns]
                yield pltpu.make_async_copy(w_ref.at[pl.ds(table.row(t, *block), size), columns], to, w_sem.at[c, at])

        def results(c):
            columns = pl.ds(c * span, span)
            yield pltpu.make_async_copy(result.at[:, columns], outs[0].at[:, columns], o_sem.at[c, 0])
            for n, out in enumerate(outs[1:]):
                part = result.at[pl.ds(n * size, size), columns]
                yield pltpu.make_async_copy(part, out.at[:, columns], o_sem.at[c, 1 + n])

        reads = [pltpu.make_async_copy(ref, more.at[n], r_sem.at[n]) for n, ref in enumerate(t_refs)]
        for copy in reads:
            copy.start()
        for c in range(chunks):
            for copy in copies(c):
                copy.start()
        for copy in reads:
            copy.wait()
        left[...] = total_of([more[n] for n in range(len(terms))])
        keep = pltpu.make_async_copy(left, r_out, r_sem.at[len(terms)])
        keep.start()
        for c in range(chunks):
            for copy in copies(c):
                copy.wait()
            columns = pl.ds(c * span, span)
            step = rate * jnp.dot(left[...], right[:, columns], preferred_element_type=F32)
            result[:, columns] = (base[:, columns].astype(F32) - step).astype(BF16)
            for copy in results(c):
                copy.start()
        for c in range(chunks):
            for copy in results(c):
                copy.wait()
        keep.wait()

    out = pl.pallas_call(
        kernel,
        grid_spec=grid_of(
            (1,),
            [ANY] * (2 + len(terms) + len(when)),
            [ANY] * (parts + 1),
            [
                pltpu.VMEM((tokens, width), BF16),
                pltpu.VMEM((rows, width), BF16),
                pltpu.VMEM((rows, tokens), BF16),
                pltpu.VMEM((len(terms), rows, tokens), BF16),
                pltpu.VMEM((rows, width), BF16),
                pltpu.SemaphoreType.DMA((chunks, len(blocks))),
                pltpu.SemaphoreType.DMA((chunks,)),
                pltpu.SemaphoreType.DMA((len(terms) + 1,)),
                pltpu.SemaphoreType.DMA((chunks, parts)),
            ],
        ),
        out_shape=[jax.ShapeDtypeStruct((rows, width), BF16)]
        + [jax.ShapeDtypeStruct((size, width), BF16)] * (parts - 1)
        + [jax.ShapeDtypeStruct((rows, tokens), BF16)],
        name="stepped_blocks",
        **options(),
    )(table.values, w, h, *terms, *when)
    return list(out[:parts]), out[parts]


def tail_rows(w, h, goals, first, count, tile, table, scale, when, held, blank):
    tokens, width = h.shape
    per = goals.shape[0]
    base = first // tile

    def kernel(t, w_ref, g_ref, h_ref, *refs):
        out, goal = refs[len(when) + len(held)], refs[-1]
        here = lax.div((base + pl.program_id(0)) * tile, per) == table.tensor(t)

        @pl.when(here)
        def _():
            goal[...] = g_ref[...].T

        @pl.when(jnp.logical_not(here))
        def _():
            goal[...] = jnp.zeros_like(goal)

        value = matmul_nt(h_ref[...], w_ref[...]) * scale
        out[...] = (value - goal[...].astype(F32)).astype(BF16)

    out = pl.pallas_call(
        kernel,
        grid_spec=grid_of(
            (count // tile,),
            [
                pl.BlockSpec((tile, width), lambda i, t: (base + i, 0)),
                pl.BlockSpec((tile, tokens), lambda i, t: (lax.rem(base + i, per // tile), 0)),
                pl.BlockSpec((tokens, width), lambda i, t: (0, 0)),
            ]
            + [ANY] * (len(when) + len(held)),
            [pl.BlockSpec((tokens, tile), lambda i, t: (0, i))] + [ANY] * (len(held) + len(blank)),
            [pltpu.VMEM((tokens, tile), BF16)],
        ),
        out_shape=[jax.ShapeDtypeStruct((tokens, count), BF16)]
        + [like(x) for x in held]
        + list(blank),
        input_output_aliases={4 + len(when) + n: 1 + n for n in range(len(held))},
        name="tail_rows",
        **options(),
    )(table.values, w, goals, h, *when, *held)
    return out[0], list(out[1 : 1 + len(held)]), list(out[1 + len(held) :])


def first_features(heads, features, when):
    tokens = heads[0].shape[1]
    frag = sum(x.shape[0] for x in heads)

    def kernel(*refs):
        out, flipped, sem = refs[-3:]
        column = 0
        for ref in refs[: len(heads)]:
            flipped[:, pl.ds(column, ref.shape[0])] = ref[...].T
            column += ref.shape[0]
        copy = pltpu.make_async_copy(flipped, out.at[:, pl.ds(0, frag)], sem)
        copy.start()
        copy.wait()

    return pl.pallas_call(
        kernel,
        grid=(1,),
        in_specs=[pl.BlockSpec(x.shape, lambda i: (0, 0)) for x in heads] + [ANY] * len(when),
        out_specs=ANY,
        out_shape=jax.ShapeDtypeStruct((tokens, features), BF16),
        scratch_shapes=[pltpu.VMEM((tokens, frag), BF16), pltpu.SemaphoreType.DMA],
        name="first_features",
        **options(),
    )(*heads, *when)


def more_features(left, column, terms, when):
    tokens, count = terms[0].shape
    step = count // 2

    def kernel(*refs):
        refs[-1][...] = total_of([ref[...] for ref in refs[: len(terms)]])

    return pl.pallas_call(
        kernel,
        grid=(2,),
        in_specs=[pl.BlockSpec((tokens, step), lambda i: (0, i))] * len(terms) + [ANY] * (1 + len(when)),
        out_specs=pl.BlockSpec((tokens, step), lambda i: (0, column // step + i)),
        out_shape=like(left),
        input_output_aliases={len(terms): 0},
        name="more_features",
        **options(),
    )(*terms, left, *when)


def outer_update(base, moment, total, islands):
    pseudo = base - total / islands
    new_momentum = outer_beta * moment + pseudo
    return base - outer_rate * (pseudo + outer_beta * new_momentum), new_momentum


def outer_step(table, s, got, stored, at, global_weights, momentum, mixed, islands, when):
    size = table.size
    rows, width = global_weights.shape

    steps = next(n for n in (4, 2, 1) if width % (n * 128) == 0)
    span = width // steps

    def kernel(t, a_ref, b_ref, s_ref, g_ref, m_ref, held, *refs):
        g_out, m_out, target, buffer, sems = refs[len(when) :]
        i = pl.program_id(0)

        def copy(i, n):
            part = pl.ds(pl.multiple_of(i * span, span), span)
            to = target.at[pl.ds(table.row(t, s, n), size), part]
            return pltpu.make_async_copy(buffer.at[pl.ds(n * size, size), part], to, sems.at[i, n])

        for n, ref in enumerate((a_ref, b_ref)):
            rows = pl.ds(n * size, size)
            own = s_ref[rows, :].astype(F32)
            new_global, new_momentum = outer_update(g_ref[rows, :], m_ref[rows, :], ref[...].astype(F32) + own, islands)
            g_out[rows, :] = new_global
            m_out[rows, :] = new_momentum
            value = mix_share * own + (1.0 - mix_share) * new_global.astype(BF16).astype(F32)
            buffer[rows, pl.ds(pl.multiple_of(i * span, span), span)] = value.astype(BF16)
            copy(i, n).start()

        @pl.when(i == steps - 1)
        def _():
            for j in range(steps):
                for n in range(2):
                    copy(j, n).wait()

    half = pl.BlockSpec((size, span), lambda i, t: (0, i))
    full = pl.BlockSpec((rows, span), lambda i, t: (0, i))
    return pl.pallas_call(
        kernel,
        grid_spec=grid_of(
            (steps,),
            [half, half, pl.BlockSpec((rows, span), lambda i, t: (at, i)), full, full, ANY] + [ANY] * len(when),
            [full, full, ANY],
            [pltpu.VMEM((rows, width), BF16), pltpu.SemaphoreType.DMA((steps, 2))],
        ),
        out_shape=[like(global_weights), like(momentum), like(mixed)],
        input_output_aliases={6: 2},
        name="outer_step",
        **options(),
    )(table.values, *got, stored, global_weights, momentum, mixed, *when)


def mix_pair(table, s, got, stored, at, mixed):
    size = table.size
    width = mixed.shape[1]

    def kernel(t, a_ref, b_ref, s_ref, held, target, buffer, sems):
        for n, ref in enumerate((a_ref, b_ref)):
            rows = pl.ds(n * size, size)
            value = mix_share * s_ref[rows, :].astype(F32) + (1.0 - mix_share) * ref[...].astype(F32)
            buffer[rows, :] = value.astype(BF16)
        copies = [
            pltpu.make_async_copy(
                buffer.at[pl.ds(n * size, size), :], target.at[pl.ds(table.row(t, s, n), size), :], sems.at[n]
            )
            for n in range(2)
        ]
        for copy in copies:
            copy.start()
        for copy in copies:
            copy.wait()

    return pl.pallas_call(
        kernel,
        grid_spec=grid_of(
            (1,),
            [pl.BlockSpec((size, width), lambda i, t: (0, 0))] * 2
            + [pl.BlockSpec((2 * size, width), lambda i, t: (at, 0)), ANY],
            ANY,
            [pltpu.VMEM((2 * size, width), BF16), pltpu.SemaphoreType.DMA((2,))],
        ),
        out_shape=like(mixed),
        input_output_aliases={4: 0},
        name="mix_pair",
        **options(58),
    )(table.values, *got, stored, mixed)


def mix_and_back(w, left, pairs, table, first, count, tile, scale, s, got, stored, at, grad_hidden, mixed):
    size = table.size
    tokens, features = left.shape
    width = w.shape[1]
    blocks = [(m, n) for m in range(pairs) for n in range(2)]
    frag = len(blocks) * size
    more = [mixed] + ([] if grad_hidden is None else [grad_hidden])

    def kernel(t, l_ref, a_ref, b_ref, s_ref, *refs):
        i = pl.program_id(0)
        out, target = refs[len(blocks) + 1 + len(more) : len(blocks) + 3 + len(more)]
        buffer, sems = refs[-2:]

        def copy(n):
            to = target.at[pl.ds(table.row(t, s, n), size), :]
            return pltpu.make_async_copy(buffer.at[pl.ds(n * size, size), :], to, sems.at[n])

        @pl.when(i == 0)
        def _():
            for n, ref in enumerate((a_ref, b_ref)):
                rows = pl.ds(n * size, size)
                value = mix_share * s_ref[rows, :].astype(F32) + (1.0 - mix_share) * ref[...].astype(F32)
                buffer[rows, :] = value.astype(BF16)
                copy(n).start()

        parts = jnp.concatenate([p[...] for p in refs[: len(blocks)]], axis=0)
        total = jnp.dot(l_ref[:, :frag], parts, preferred_element_type=F32)
        total += jnp.dot(l_ref[:, frag:], refs[len(blocks)][...], preferred_element_type=F32)
        out[...] = (total * scale).astype(BF16)

        @pl.when(i == count - 1)
        def _():
            copy(0).wait()
            copy(1).wait()

    operands = 5 + len(blocks) + 1
    aliases = {operands: 1}
    if grad_hidden is not None:
        aliases[operands + 1] = 0

    def block_spec(m, n):
        return pl.BlockSpec((size, tile), lambda i, t: (table.block(t, m, n), first + i))

    rest = pl.BlockSpec((pl.Element(features - frag), pl.Element(tile)), lambda i, t: (frag, (first + i) * tile))
    return pl.pallas_call(
        kernel,
        grid_spec=grid_of(
            (count,),
            [pl.BlockSpec((tokens, features), lambda i, t: (0, 0))]
            + [pl.BlockSpec((size, width), lambda i, t: (0, 0))] * 2
            + [pl.BlockSpec((2 * size, width), lambda i, t: (at, 0))]
            + [block_spec(*x) for x in blocks]
            + [rest]
            + [ANY] * len(more),
            [pl.BlockSpec((tokens, tile), lambda i, t: (0, first + i)), ANY],
            [pltpu.VMEM((2 * size, width), BF16), pltpu.SemaphoreType.DMA((2,))],
        ),
        out_shape=[jax.ShapeDtypeStruct((tokens, width), BF16), like(mixed)],
        input_output_aliases=aliases,
        name="mix_and_back",
        **options(58),
    )(table.values, left, *got, stored, *([w] * (len(blocks) + 1)), *more)


def shards(hidden, island_weights, targets, global_weights, momentum):
    h = hidden[0]
    w = island_weights[0]
    goals = targets[0]
    islands = lax.axis_size("island")
    tensors = lax.axis_size("tensor")
    island = lax.axis_index("island")
    tensor = lax.axis_index("tensor")
    rows = global_weights.shape[0]
    size = rows // 2
    frag = rows * islands
    width = w.shape[1]
    scale = 1.0 / math.sqrt(width * tensors)
    rate = inner_rate * scale
    per = goals.shape[0]

    def island_at(k):
        return jnp.where(k < islands // 2, 2 * k, 2 * (islands - 1 - k) + 1)

    def number_at(k):
        return 2 * k if k < islands // 2 else 2 * (islands - 1 - k) + 1

    place = jnp.where(island % 2 == 0, island // 2, islands - 1 - island // 2)
    ahead = [(number_at(k), number_at((k + 1) % islands)) for k in range(islands)]
    back = [(b, a) for a, b in ahead]
    starts = [island_at(lax.rem(place + k, islands)) * rows for k in range(islands)]

    pairs = [(starts[(-s - 1) % islands], starts[(s + 1) % islands] + size) for s in range(islands)]
    table = Table(pairs, tensor, size, per)

    early = 3
    (x,), _ = partial_blocks(w, h, goals, 0, 1, table, scale)
    bit = tensors // 2
    while bit > 1:
        x = add(x, across(x, tensors, bit))
        bit //= 2
    first_terms = [x, across(x, tensors, 1)]
    (x,), _ = partial_blocks(w, h, goals, 1, early, table, scale)
    next_terms = terms_of(x, tensors)
    (first_store, *acc), first_residue = stepped_blocks(w, h, first_terms, 0, 1, table, rate, [], True)

    tile = min(512, per)
    tail_rest = w.shape[0] - frag
    calls = next(n for n in (3, 1) if tail_rest % (n * tile) == 0)
    tail_at = {1: 0, 3: 1, 4: 2}
    tail_due = {5: [0], 6: [1]}
    chips_due = {3: 0, 5: 1}
    tails = []
    mixed = None
    store = {}

    for s in range(islands - 1):
        got = [lax.ppermute(acc[0], "island", ahead), lax.ppermute(acc[1], "island", back)]
        name, at = ("next", s) if s < early else ("last", s - early)
        order = acc
        if s == 0:
            (x,), _ = partial_blocks(w, h, goals, 1 + early, islands - 1 - early, table, scale, order)
            last_terms = terms_of(x, tensors)
            order = [x]
            (store["next"],), next_residue = stepped_blocks(
                w, h, next_terms, 1, early, table, rate, order, False
            )
        if s == early - 1:
            (store["last"],), last_residue = stepped_blocks(
                w, h, last_terms, 1 + early, islands - 1 - early, table, rate, order, False
            )
            order = [last_residue]
        if tail_at.get(s, calls) < calls:
            count = tail_rest // calls
            blank = [jax.ShapeDtypeStruct((frag, width), BF16)] if mixed is None else []
            x, _, fresh = tail_rows(
                w, h, goals, frag + tail_at[s] * count, count, tile, table, scale, order, [], blank
            )
            mixed = fresh[0] if fresh else mixed
            tails.append(terms_of(x, tensors))
            order = [x]
            last_tail = x
        if s == 5:
            left = first_features([first_residue, next_residue, last_residue], w.shape[0], order)
            order = [left]
        for n in tail_due.get(s, []):
            left = more_features(left, frag + n * tails[n][0].shape[1], tails[n], [] if s == 5 else order)
            order = [left]
        if order is not acc and s > 0:
            due = [tails[chips_due[s]][1]] if chips_due.get(s, len(tails)) < len(tails) else []
            (store[name],) = join([store[name]], *order, *due)
        own = [lax.slice_in_dim(store[name], (2 * at + n) * size, (2 * at + n + 1) * size, axis=0) for n in range(2)]
        if s < islands - 2:
            acc = [add(got[i], own[i]) for i in range(2)]
    send = []
    for n in range(2):
        base, moment = (lax.slice_in_dim(x, n * size, (n + 1) * size, axis=0) for x in (global_weights, momentum))
        send.append(outer_update(base, moment, got[n].astype(F32) + own[n].astype(F32), islands)[0].astype(BF16))

    def stored(s):
        if s == 0:
            return first_store, 0
        return (store["next"], s - 1) if s <= early else (store["last"], s - 1 - early)

    wide = 256 if width % 256 == 0 else 128
    tiles = width // wide
    pieces = min(5, tiles, islands - 3)
    cuts = [-(-tiles * n // pieces) for n in range(pieces + 1)]
    grad_hidden = None

    new_global, new_momentum, mixed = outer_step(
        table, islands - 1, got, *stored(islands - 1), global_weights, momentum, mixed, islands, send
    )
    later = range(sum(len(x) for x in tail_due.values()), len(tails))
    waiting = []
    for s in range(islands - 1):
        send = [lax.ppermute(send[0], "island", ahead), lax.ppermute(send[1], "island", back)]
        if s == 0:
            send = join(send, mixed)
        if waiting:
            send = [*join(send[:1], *waiting), send[1]]
        piece = s - (islands - 2 - pieces)
        if 0 <= piece < pieces:
            grad_hidden, mixed = mix_and_back(
                w, left, islands, table, cuts[piece], cuts[piece + 1] - cuts[piece], wide, scale, s, send, *stored(s),
                grad_hidden, mixed,
            )
            waiting = [mixed]
        else:
            mixed = mix_pair(table, s, send, *stored(s), mixed)
        if s == 0 and later:
            terms = terms_of(last_tail, tensors, send)
            for n in later:
                left = more_features(left, frag + n * terms[0].shape[1], terms, [mixed])
            waiting = [mixed, left]
    return (mixed[None], new_global, new_momentum, grad_hidden[None])


def solution(mesh):
    return jax.shard_map(
        shards,
        mesh=mesh,
        in_specs=(
            P("island", None, "tensor"),
            P("island", None, "tensor"),
            P("island", "tensor", None),
            P("island", "tensor"),
            P("island", "tensor"),
        ),
        out_specs=(
            P("island", None, "tensor"),
            P("island", "tensor"),
            P("island", "tensor"),
            P("island", None, "tensor"),
        ),
        check_vma=False,
    )
```
